32 devices in a mesh: pts: 8 (over y, x, core), lists: 4 (over z).
Axes of the slice: x: 2, y: 2, z: 4, core: 2. Of those that a mesh axis runs over, the one named last changes fastest.
Arguments:
- points: bfloat16 [3072, 256], P('pts'), may hold values from -4 to 4
- centroids: bfloat16 [16384, 256], P('lists'), may hold values from -0.375 to 0.375
- prior: int32 [3072], P('pts'), may hold values from 0 to 16383
- loads: int32 [16384], P('lists'), may hold values from 2 to 14, as said below
Outputs:
- centroid_means: float32 [256, 16384], P('pts', 'lists')
- log_col_scale: float32 [16384], P('lists')
The draws below stay inside these ranges and needn't reach their ends.
Inputs may be any that keep to these rules, and one draw needn't show every extreme that they name: Lists 2k and 2k + 1 have loads 8 + e and 8 - e for some e of 0 to 6, so all loads sum to 131072.
All inputs are finite; a program needn't handle non-finite values.
Results may differ from the reference program's by a relative error of at most 0.003.
Values sent between devices are 32-bit elements; how exact they have to be, the bound alone decides.
A program may use at most 64 MiB of HBM per device.

```python
import jax
import jax.numpy as jnp
from jax import lax

DIM = 256
ITERS = 3
BLOCK = 512
LISTS = 16384
NPTS = 3072


def draw_loads(key, part):
    spread = jax.random.randint(key, (LISTS // 2,), 0, 7).astype(jnp.int32)
    return jnp.stack([8 + spread, 8 - spread], axis=1).reshape(LISTS).astype(jnp.int32)


def place_ends(result, rng, smallest, largest):
    extent = result.shape
    index_at = [jax.random.randint(jax.random.fold_in(rng, axis), (), 0, extent[axis]) for axis in range(len(extent))]
    result = result.at[tuple(index_at)].set(smallest)
    longest = extent.index(max(extent))
    index_at[longest] = (index_at[longest] + 1) % extent[longest]
    return result.at[tuple(index_at)].set(largest)


def shard_levels(key, shape, split, least, high):
    factor_of, own = 1.0, jax.random.fold_in(key, 6)
    for axis_at, shards_of in split:
        draws = jnp.exp(jax.random.uniform(jax.random.fold_in(own, axis_at), (shards_of,), jnp.float32, least / len(split), high / len(split)))
        factor_of = factor_of * jnp.repeat(draws, shape[axis_at] // shards_of).reshape([-1 if axis == axis_at else 1 for axis in range(len(shape))])
    return factor_of


def centred(stream_key, shape, deviation, reach, shards=(), dtype=jnp.bfloat16):
    level = shard_levels(stream_key, shape, shards, -0.22, 0.18) if shards else 1.0
    array = jax.random.normal(stream_key, shape, jnp.float32) * deviation * level
    return jnp.minimum(jnp.maximum(array, -reach), reach).astype(dtype)


def setup_inputs(seed: int = 0) -> dict:
    streams_of = jax.random.split(jax.random.key(seed), 5)
    return {
        "points": centred(streams_of[0], (NPTS, DIM), 1.0, 4.0, ((0, 8),)),
        "centroids": centred(streams_of[1], (LISTS, DIM), DIM ** -0.5, 0.375, ((0, 4),)),
        "prior": place_ends(jax.random.randint(streams_of[2], (NPTS,), 0, LISTS), jax.random.fold_in(streams_of[2], 1), 0, LISTS - 1).astype(jnp.int32),
        "loads": draw_loads(jax.random.fold_in(streams_of[4], 71), 0),
    }


def kernel_tile(points, cent_block, prior, start):
    score = lax.dot_general(points, cent_block, (((1,), (1,)), ((), ())), preferred_element_type=jnp.float32)
    cols = start + lax.iota(jnp.int32, cent_block.shape[0])
    hit = (prior[:, None] == cols[None, :]).astype(jnp.float32)
    return jnp.exp(3.0 * score + 10.0 * hit)


def reference(points, centroids, prior, loads):
    count = LISTS // BLOCK
    target = loads.astype(jnp.float32) * (NPTS / (8.0 * LISTS))
    starts = (jnp.arange(count) * BLOCK).astype(jnp.int32)

    def tile(start):
        block = lax.dynamic_slice_in_dim(centroids, start, BLOCK, 0)
        return kernel_tile(points, block, prior, start)

    col_scale = jnp.ones((LISTS,), jnp.float32)
    row_scale = jnp.ones((NPTS,), jnp.float32)
    for step in range(ITERS):
        def add_rows(carry, start):
            part = lax.dynamic_slice_in_dim(col_scale, start, BLOCK, 0)
            return carry + jnp.sum(tile(start) * part[None, :], axis=1), None

        row_total, _ = lax.scan(add_rows, jnp.zeros((NPTS,), jnp.float32), starts)
        row_scale = 1.0 / row_total
        col_total = lax.map(lambda start: jnp.sum(tile(start) * row_scale[:, None], axis=0), starts).reshape(LISTS)
        col_scale = target / col_total

    def sums_of(start):
        part = lax.dynamic_slice_in_dim(col_scale, start, BLOCK, 0)
        plan = (tile(start) * row_scale[:, None] * part[None, :]).astype(jnp.bfloat16)
        return lax.dot_general(points, plan, (((0,), (0,)), ((), ())), preferred_element_type=jnp.float32)

    sums = lax.map(sums_of, starts)
    sums = jnp.transpose(sums, (1, 0, 2)).reshape(DIM, LISTS)
    return sums / target[None, :], jnp.log(col_scale)
```

```python
import functools

import jax
import jax.numpy as jnp
from jax import lax
from jax.experimental import pallas as pl
from jax.experimental.pallas import tpu as pltpu

from jax.sharding import PartitionSpec as P

ITERS = 3
BLOCK = 512
LANES = 128
MESH = pl.DeviceIdType.MESH
NT = (((1,), (1,)), ((), ()))


def spread(row):
    return jnp.broadcast_to(row, (LANES, LANES)).T


def gather_up(block):
    return jnp.sum(block.T, axis=0, keepdims=True)


def kernel(
    n,
    nl,
    scale,
    pts_ref,
    cent_ref,
    prior_ref,
    loads_ref,
    out_ref,
    log_ref,
    mass,
    mass_t,
    allp,
    pts_t,
    plan_t,
    near,
    rowb,
    rowacc,
    col,
    row_out,
    row_in,
    col_out,
    col_in,
    row_all,
    sums,
    log_all,
    row_send,
    row_recv,
    col_send,
    col_recv,
    ag_send,
    ag_recv,
    fw_send,
    fw_recv,
    ra_send,
    ra_recv,
    out_send,
    out_recv,
    log_send,
    log_recv,
):
    p = lax.axis_index("pts")
    z = lax.axis_index("lists")
    m = pts_ref.shape[0]
    lists = cent_ref.shape[0]
    tiles = lists // LANES
    chunks = m // LANES
    share = lists // n
    share_tiles = share // LANES
    half = n // 2
    sibling = p + 1 - 2 * lax.rem(p, 2)

    def pt(k):
        return lax.rem(p + k, n)

    barrier = pltpu.get_barrier_semaphore()
    for k in range(1, n):
        pl.semaphore_signal(barrier, inc=1, device_id={"pts": pt(k)}, device_id_type=MESH)
    for k in range(1, nl):
        pl.semaphore_signal(
            barrier, inc=1, device_id={"lists": lax.rem(z + k, nl)}, device_id_type=MESH
        )

    allp[p, :m, :] = pts_ref[...].astype(jnp.float32)
    allp[p, m:, :] = jnp.zeros((8, allp.shape[2]), jnp.float32)
    row_out[...] = jnp.zeros_like(row_out)
    log_all[p] = jnp.zeros(log_all.shape[1:], jnp.float32)
    for r in range(chunks):
        prior_row = prior_ref[r : r + 1, :].astype(jnp.float32)
        allp[p, m + r : m + r + 1, 0:LANES] = prior_row
        near[r * LANES : (r + 1) * LANES, :] = spread(prior_row - (z * lists).astype(jnp.float32))
    pl.semaphore_wait(barrier, n - 1 + nl - 1)

    def remote(src, dst, send, recv, where):
        copy = pltpu.make_async_remote_copy(
            src_ref=src, dst_ref=dst, send_sem=send, recv_sem=recv,
            device_id=where, device_id_type=MESH,
        )
        copy.start()
        return copy

    started = []
    gathers = [remote(allp.at[p], allp.at[p], ag_send.at[0], ag_recv.at[0], {"pts": sibling})]
    for k in range(1, half):
        gathers.append(
            remote(allp.at[p], allp.at[p], ag_send.at[k], ag_recv.at[k], {"pts": pt(2 * k)})
        )
    started += gathers

    rowacc[...] = jnp.zeros_like(rowacc)
    per = BLOCK // LANES
    lane = lax.broadcasted_iota(jnp.int32, (m, LANES), 1).astype(jnp.float32)

    def make(b, carry):
        score = lax.dot_general(
            pts_ref[...], cent_ref[pl.ds(pl.multiple_of(b * BLOCK, BLOCK), BLOCK), :], NT,
            preferred_element_type=jnp.float32,
        )
        rel = near[...] - (b * BLOCK).astype(jnp.float32)
        total = rowacc[...]
        for c in range(per):
            hit = jnp.where(rel == lane + float(c * LANES), 10.0, 0.0)
            value = jnp.exp(3.0 * score[:, c * LANES : (c + 1) * LANES] + hit)
            mass[b * per + c] = value
            total = total + value
        rowacc[...] = total
        return carry

    lax.fori_loop(0, lists // BLOCK, make, 0)

    def send_rows(step):
        for r in range(chunks):
            row_out[step, r : r + 1, :] = gather_up(rowacc[r * LANES : (r + 1) * LANES, :])
        copies = [
            remote(
                row_out.at[step], row_in.at[step, k], row_send.at[step, k], row_recv.at[step, k],
                {"lists": lax.rem(z + k, nl)},
            )
            for k in range(1, nl)
        ]
        started.extend(copies)
        return copies

    def take_rows(step, copies):
        total = row_out[step]
        for k, copy in enumerate(copies, 1):
            copy.wait_recv()
            total = total + row_in[step, k]
        return 1.0 / total

    def send_cols(step, row):
        for r in range(chunks):
            rowb[r * LANES : (r + 1) * LANES, :] = spread(row[r : r + 1, :])

        def add(t, carry):
            col_out[step, pl.ds(t, 1), :] = jnp.sum(mass[t] * rowb[...], axis=0, keepdims=True)
            return carry

        lax.fori_loop(0, tiles, add, 0, unroll=4)
        copies = [
            remote(
                col_out.at[step], col_in.at[step, k], col_send.at[step, k], col_recv.at[step, k],
                {"pts": pt(k)},
            )
            for k in range(1, n)
        ]
        started.extend(copies)
        return copies

    def take_cols(step, copies):
        total = col_out[step]
        for k, copy in enumerate(copies, 1):
            copy.wait_recv()
            total = total + col_in[step, k]
        col[...] = loads_ref[...].astype(jnp.float32) * scale / total

    def add_rows():
        for r in range(chunks):
            part = pl.ds(r * LANES, LANES)

            def add(t, acc):
                return acc + mass[t, part, :] * col[pl.ds(t, 1), :]

            rowacc[part, :] = lax.fori_loop(
                0, tiles, add, jnp.zeros((LANES, LANES), jnp.float32), unroll=4
            )

    own = pl.multiple_of(p * share, share)
    first = (z * lists + p * share).astype(jnp.float32)
    index = lax.broadcasted_iota(jnp.int32, (share, LANES), 0).astype(jnp.float32) + first

    def part_of(s):
        piece = allp[s, :m, :]
        pts_t[:, pl.ds(pl.multiple_of(s * m, LANES), m)] = piece.T.astype(jnp.bfloat16)
        score = lax.dot_general(
            cent_ref[pl.ds(own, share), :], piece.astype(jnp.bfloat16), NT,
            preferred_element_type=jnp.float32,
        )
        for r in range(chunks):
            hit = jnp.where(index == allp[s, m + r : m + r + 1, 0:LANES], 10.0, 0.0)
            mass_t[s * chunks + r] = jnp.exp(3.0 * score[:, r * LANES : (r + 1) * LANES] + hit)

    copies = send_rows(0)
    part_of(p)
    row = take_rows(0, copies)
    copies = send_cols(0, row)
    gathers[0].wait_recv()
    part_of(sibling)
    take_cols(0, copies)
    add_rows()
    row = take_rows(1, send_rows(1))
    take_cols(1, send_cols(1, row))
    add_rows()
    copies = send_rows(2)
    forwards = []
    for k in range(1, half):
        gathers[k].wait_recv()
        source = pt(n - 2 * k)
        forwards.append(
            remote(
                allp.at[source], allp.at[source], fw_send.at[k], fw_recv.at[k], {"pts": sibling}
            )
        )
    started += forwards
    row_all[p] = take_rows(2, copies)
    copies = [
        remote(row_all.at[p], row_all.at[p], ra_send.at[k], ra_recv.at[k], {"pts": pt(k)})
        for k in range(1, n)
    ]
    started += copies

    def direct(k, carry):
        part_of(lax.rem(p + n - 2 * k, n))
        return carry

    lax.fori_loop(1, half, direct, 0)
    for copy in forwards:
        copy.wait_recv()

    def relayed(k, carry):
        part_of(lax.rem(sibling + n - 2 * k, n))
        return carry

    lax.fori_loop(1, half, relayed, 0)
    for copy in copies:
        copy.wait_recv()

    for c in range(share_tiles):
        part = pl.ds(c * LANES, LANES)

        def add(s, acc):
            for r in range(chunks):
                acc = acc + mass_t[s * chunks + r, part, :] * row_all[s, r : r + 1, :]
            return acc

        acc = lax.fori_loop(0, n, add, jnp.zeros((LANES, LANES), jnp.float32))
        total = jnp.sum(acc, axis=1, keepdims=True)
        target = loads_ref[pl.ds(p * share_tiles + c, 1), :].astype(jnp.float32) * scale
        colb = spread(target) / total
        log_all[p, c : c + 1, :] = jnp.log(colb).T[0:1, :]

        def plan(s, carry):
            for r in range(chunks):
                value = mass_t[s * chunks + r, part, :] * row_all[s, r : r + 1, :] * colb
                plan_t[part, pl.ds(pl.multiple_of(s * m + r * LANES, LANES), LANES)] = value.astype(
                    jnp.bfloat16
                )
            return carry

        lax.fori_loop(0, n, plan, 0)
    copies = [
        remote(log_all.at[p], log_all.at[p], log_send.at[k], log_recv.at[k], {"pts": pt(k)})
        for k in range(1, n)
    ]
    total = lax.dot_general(pts_t[...], plan_t[...], NT, preferred_element_type=jnp.float32)
    depth = out_ref.shape[0]
    for c in range(share_tiles):
        target = loads_ref[pl.ds(p * share_tiles + c, 1), :].astype(jnp.float32) * scale
        part = total[:, c * LANES : (c + 1) * LANES] / target
        for q in range(n):
            sums[q, :, c * LANES : (c + 1) * LANES] = part[q * depth : (q + 1) * depth, :]
    copies += [
        remote(
            sums.at[pt(k)], out_ref.at[:, pl.ds(own, share)], out_send.at[k], out_recv.at[k],
            {"pts": pt(k)},
        )
        for k in range(1, n)
    ]
    out_ref[:, pl.ds(own, share)] = sums[p]
    for copy in copies:
        copy.wait_recv()
    for s in range(n):
        log_ref[s * share_tiles : (s + 1) * share_tiles, :] = log_all[s, :share_tiles, :]
    for copy in started + copies:
        copy.wait_send()


def local(n, nl, points, centroids, prior, loads):
    m, dim = points.shape
    lists = centroids.shape[0]
    tiles = lists // LANES
    chunks = m // LANES
    share = lists // n
    scale = (m * n) / (8.0 * lists * nl)
    f32 = jnp.float32
    dma = pltpu.SemaphoreType.DMA
    out, log = pl.pallas_call(
        functools.partial(kernel, n, nl, scale),
        out_shape=(
            jax.ShapeDtypeStruct((dim // n, lists), f32),
            jax.ShapeDtypeStruct((tiles, LANES), f32),
        ),
        in_specs=[pl.BlockSpec(memory_space=pltpu.VMEM)] * 4,
        out_specs=[pl.BlockSpec(memory_space=pltpu.VMEM)] * 2,
        scratch_shapes=[
            pltpu.VMEM((tiles, m, LANES), f32),
            pltpu.VMEM((n * chunks, share, LANES), f32),
            pltpu.VMEM((n, m + 8, dim), f32),
            pltpu.VMEM((dim, n * m), jnp.bfloat16),
            pltpu.VMEM((share, n * m), jnp.bfloat16),
            pltpu.VMEM((m, LANES), f32),
            pltpu.VMEM((m, LANES), f32),
            pltpu.VMEM((m, LANES), f32),
            pltpu.VMEM((tiles, LANES), f32),
            pltpu.VMEM((ITERS, 8, LANES), f32),
            pltpu.VMEM((ITERS, nl, 8, LANES), f32),
            pltpu.VMEM((ITERS - 1, tiles, LANES), f32),
            pltpu.VMEM((ITERS - 1, n, tiles, LANES), f32),
            pltpu.VMEM((n, 8, LANES), f32),
            pltpu.VMEM((n, dim // n, share), f32),
            pltpu.VMEM((n, 8, LANES), f32),
            dma((ITERS, nl)),
            dma((ITERS, nl)),
            dma((ITERS - 1, n)),
            dma((ITERS - 1, n)),
            dma((n // 2,)),
            dma((n // 2,)),
            dma((n // 2,)),
            dma((n // 2,)),
            dma((n,)),
            dma((n,)),
            dma((n,)),
            dma((n,)),
            dma((n,)),
            dma((n,)),
        ],
        compiler_params=pltpu.CompilerParams(
            collective_id=0, has_side_effects=True, vmem_limit_bytes=56 * 1024 * 1024
        ),
    )(points, centroids, prior.reshape(chunks, LANES), loads.reshape(tiles, LANES))
    return out, log.reshape(lists)


def solution(mesh):
    return jax.shard_map(
        functools.partial(local, mesh.shape["pts"], mesh.shape["lists"]),
        mesh=mesh,
        in_specs=(P("pts", None), P("lists", None), P("pts"), P("lists")),
        out_specs=(P("pts", "lists"), P("lists")),
        check_vma=False,
    )
```

```python
import functools

import jax
import jax.numpy as jnp
from jax import lax
from jax.experimental import pallas as pl
from jax.experimental.pallas import tpu as pltpu

from jax.sharding import PartitionSpec as P

ITERS = 3
BLOCK = 512
LANES = 128
MESH = pl.DeviceIdType.MESH
NT = (((1,), (1,)), ((), ()))


def spread(row):
    return jnp.broadcast_to(row, (LANES, LANES)).T


def gather_up(block):
    return jnp.sum(block.T, axis=0, keepdims=True)


def kernel(
    n,
    nl,
    scale,
    paced,
    group,
    pts_ref,
    cent_hbm,
    prior_ref,
    loads_ref,
    out_ref,
    log_ref,
    mass,
    mass_t,
    allp,
    pts_t,
    plan_t,
    near,
    rowb,
    rowacc,
    col,
    row_out,
    row_in,
    col_out,
    col_in,
    row_all,
    sums,
    log_all,
    row_send,
    row_recv,
    col_send,
    col_recv,
    ag_send,
    ag_recv,
    fw_send,
    fw_recv,
    ra_send,
    ra_recv,
    out_send,
    out_recv,
    log_send,
    log_recv,
    cent_ref,
    cent_sem,
):
    p = lax.axis_index("pts")
    z = lax.axis_index("lists")
    m = pts_ref.shape[0]
    lists = cent_ref.shape[0]
    tiles = lists // LANES
    chunks = m // LANES
    share = lists // n
    share_tiles = share // LANES
    half = n // 2
    sibling = p + 1 - 2 * lax.rem(p, 2)

    def pt(k):
        return lax.rem(p + k, n)

    fetch = pltpu.make_async_copy(cent_hbm, cent_ref, cent_sem)
    fetch.start()
    barrier = pltpu.get_barrier_semaphore()
    for k in range(1, n):
        pl.semaphore_signal(barrier, inc=1, device_id={"pts": pt(k)}, device_id_type=MESH)
    for k in range(1, nl):
        pl.semaphore_signal(
            barrier, inc=1, device_id={"lists": lax.rem(z + k, nl)}, device_id_type=MESH
        )

    allp[p, :m, :] = pts_ref[...].astype(jnp.float32)
    allp[p, m:, :] = jnp.zeros((8, allp.shape[2]), jnp.float32)
    row_out[...] = jnp.zeros_like(row_out)
    log_all[p] = jnp.zeros(log_all.shape[1:], jnp.float32)
    for r in range(chunks):
        prior_row = prior_ref[r : r + 1, :].astype(jnp.float32)
        allp[p, m + r : m + r + 1, 0:LANES] = prior_row
        near[r * LANES : (r + 1) * LANES, :] = spread(prior_row - (z * lists).astype(jnp.float32))
    pl.semaphore_wait(barrier, n - 1 + nl - 1)

    def remote(src, dst, send, recv, where):
        copy = pltpu.make_async_remote_copy(
            src_ref=src, dst_ref=dst, send_sem=send, recv_sem=recv,
            device_id=where, device_id_type=MESH,
        )
        copy.start()
        return copy

    started = []

    def send_piece(source, rows, send, recv, where):
        copy = remote(allp.at[source, rows], allp.at[source, rows], send, recv, {"pts": where})
        started.append(copy)
        return copy

    whole = pl.ds(0, m + 8)
    near_sib = send_piece(p, whole, ag_send.at[0], ag_recv.at[0], sibling)
    if paced:
        over_x = p + 2 - 4 * lax.rem(p // 2, 2)
        over_y = p + 4 - 8 * lax.rem(p // 4, 2)
        across = over_x + 4 - 8 * lax.rem(p // 4, 2)
        first_rows, last_rows = pl.ds(0, m // 2), pl.ds(m // 2, m // 2 + 8)
        head = [
            send_piece(p, first_rows, ag_send.at[1], ag_recv.at[1], over_x),
            send_piece(p, first_rows, ag_send.at[2], ag_recv.at[2], over_y),
        ]
    else:
        gathers = [
            send_piece(p, whole, ag_send.at[k], ag_recv.at[k], pt(2 * k)) for k in range(1, half)
        ]

    rowacc[...] = jnp.zeros_like(rowacc)
    per = BLOCK // LANES
    lane = lax.broadcasted_iota(jnp.int32, (m, LANES), 1).astype(jnp.float32)

    def make(b, carry):
        score = lax.dot_general(
            pts_ref[...], cent_ref[pl.ds(pl.multiple_of(b * BLOCK, BLOCK), BLOCK), :], NT,
            preferred_element_type=jnp.float32,
        )
        rel = near[...] - (b * BLOCK).astype(jnp.float32)
        total = rowacc[...]
        for c in range(per):
            hit = jnp.where(rel == lane + float(c * LANES), 10.0, 0.0)
            value = jnp.exp(3.0 * score[:, c * LANES : (c + 1) * LANES] + hit)
            mass[b * per + c] = value
            total = total + value
        rowacc[...] = total
        return carry

    fetch.wait()
    lax.fori_loop(0, lists // BLOCK, make, 0)

    def send_rows(step):
        for r in range(chunks):
            row_out[step, r : r + 1, :] = gather_up(rowacc[r * LANES : (r + 1) * LANES, :])
        copies = [
            remote(
                row_out.at[step], row_in.at[step, k], row_send.at[step, k], row_recv.at[step, k],
                {"lists": lax.rem(z + k, nl)},
            )
            for k in range(1, nl)
        ]
        started.extend(copies)
        return copies

    def take_rows(step, copies):
        total = row_out[step]
        for k, copy in enumerate(copies, 1):
            copy.wait_recv()
            total = total + row_in[step, k]
        return 1.0 / total

    def send_cols(step, row):
        for r in range(chunks):
            rowb[r * LANES : (r + 1) * LANES, :] = spread(row[r : r + 1, :])

        def add(t, carry):
            col_out[step, pl.ds(t, 1), :] = jnp.sum(mass[t] * rowb[...], axis=0, keepdims=True)
            return carry

        lax.fori_loop(0, tiles, add, 0, unroll=4)
        copies = [
            remote(
                col_out.at[step], col_in.at[step, k], col_send.at[step, k], col_recv.at[step, k],
                {"pts": pt(k)},
            )
            for k in range(1, n)
        ]
        started.extend(copies)
        return copies

    def take_cols(step, copies):
        total = col_out[step]
        for k, copy in enumerate(copies, 1):
            copy.wait_recv()
            total = total + col_in[step, k]
        col[...] = loads_ref[...].astype(jnp.float32) * scale / total

    def add_rows():
        for r in range(chunks):
            part = pl.ds(r * LANES, LANES)

            def add(t, acc):
                return acc + mass[t, part, :] * col[pl.ds(t, 1), :]

            rowacc[part, :] = lax.fori_loop(
                0, tiles, add, jnp.zeros((LANES, LANES), jnp.float32), unroll=4
            )

    own = pl.multiple_of(p * share, share)
    first = (z * lists + p * share).astype(jnp.float32)
    index = lax.broadcasted_iota(jnp.int32, (share, LANES), 0).astype(jnp.float32) + first

    def part_of(s):
        piece = allp[s, :m, :]
        pts_t[:, pl.ds(pl.multiple_of(s * m, LANES), m)] = piece.T.astype(jnp.bfloat16)
        score = lax.dot_general(
            cent_ref[pl.ds(own, share), :], piece.astype(jnp.bfloat16), NT,
            preferred_element_type=jnp.float32,
        )
        for r in range(chunks):
            hit = jnp.where(index == allp[s, m + r : m + r + 1, 0:LANES], 10.0, 0.0)
            mass_t[s * chunks + r] = jnp.exp(3.0 * score[:, r * LANES : (r + 1) * LANES] + hit)

    copies = send_rows(0)
    part_of(p)
    row = take_rows(0, copies)
    copies = send_cols(0, row)
    near_sib.wait_recv()
    part_of(sibling)
    take_cols(0, copies)
    if paced:
        tail = [
            send_piece(p, last_rows, ag_send.at[3], ag_recv.at[3], over_x),
            send_piece(p, last_rows, ag_send.at[4], ag_recv.at[4], over_y),
        ]
    add_rows()
    row = take_rows(1, send_rows(1))
    take_cols(1, send_cols(1, row))
    if paced:
        for copy in head + tail:
            copy.wait_recv()
        on = [
            send_piece(over_x, first_rows, ag_send.at[5], ag_recv.at[5], over_y),
            send_piece(over_y, last_rows, ag_send.at[6], ag_recv.at[6], over_x),
        ]
        forwards = [
            send_piece(over_x, whole, fw_send.at[1], fw_recv.at[1], sibling),
            send_piece(over_y, whole, fw_send.at[2], fw_recv.at[2], sibling),
        ]
    add_rows()
    copies = send_rows(2)
    if not paced:
        forwards = []
        for k in range(1, half):
            gathers[k - 1].wait_recv()
            source = pt(n - 2 * k)
            forwards.append(send_piece(source, whole, fw_send.at[k], fw_recv.at[k], sibling))
    row_all[p] = take_rows(2, copies)
    copies = [
        remote(row_all.at[p], row_all.at[p], ra_send.at[k], ra_recv.at[k], {"pts": pt(k)})
        for k in range(1, n)
    ]
    started += copies
    if paced:

        def pair(first, second):
            def one(k, carry):
                part_of(first + k * (second - first))
                return carry

            lax.fori_loop(0, 2, one, 0)

        pair(over_x, over_y)
        for copy in on:
            copy.wait_recv()
        forwards.append(send_piece(across, whole, fw_send.at[3], fw_recv.at[3], sibling))
        for copy in forwards[:2]:
            copy.wait_recv()
        across_sib = across + 1 - 2 * lax.rem(p, 2)
        pair(over_x + sibling - p, over_y + sibling - p)
        part_of(across)
        forwards[2].wait_recv()
        part_of(across_sib)
    else:

        def direct(k, carry):
            part_of(lax.rem(p + n - 2 * k, n))
            return carry

        lax.fori_loop(1, half, direct, 0)
        for copy in forwards:
            copy.wait_recv()

        def relayed(k, carry):
            part_of(lax.rem(sibling + n - 2 * k, n))
            return carry

        lax.fori_loop(1, half, relayed, 0)
    for copy in copies:
        copy.wait_recv()

    depth = out_ref.shape[0]
    order = [k for k in range(1, n)][::-1]
    copies = []

    def finish(g):
        width = group * LANES
        for c in range(g * group, (g + 1) * group):
            part = pl.ds(c * LANES, LANES)

            def add(s, acc):
                for r in range(chunks):
                    acc = acc + mass_t[s * chunks + r, part, :] * row_all[s, r : r + 1, :]
                return acc

            acc = lax.fori_loop(0, n, add, jnp.zeros((LANES, LANES), jnp.float32), unroll=2)
            total = jnp.sum(acc, axis=1, keepdims=True)
            target = loads_ref[pl.ds(p * share_tiles + c, 1), :].astype(jnp.float32) * scale
            colb = spread(target) / total
            log_all[p, c : c + 1, :] = jnp.log(colb).T[0:1, :]

            def plan(s, carry):
                for r in range(chunks):
                    value = mass_t[s * chunks + r, part, :] * row_all[s, r : r + 1, :] * colb
                    spot = pl.ds(pl.multiple_of(s * m + r * LANES, LANES), LANES)
                    plan_t[part, spot] = value.astype(jnp.bfloat16)
                return carry

            lax.fori_loop(0, n, plan, 0, unroll=2)
        total = lax.dot_general(
            pts_t[...], plan_t[g * width : (g + 1) * width, :], NT,
            preferred_element_type=jnp.float32,
        )
        for c in range(group):
            target = loads_ref[
                pl.ds(p * share_tiles + g * group + c, 1), :
            ].astype(jnp.float32) * scale
            part = total[:, c * LANES : (c + 1) * LANES] * (1.0 / target)
            for q in range(n):
                sums[g, q, :, c * LANES : (c + 1) * LANES] = part[q * depth : (q + 1) * depth, :]
        spot = pl.ds(pl.multiple_of(p * share + g * width, LANES), width)
        for k in order:
            copies.append(
                remote(
                    sums.at[g, pt(k)], out_ref.at[:, spot], out_send.at[g, k], out_recv.at[g, k],
                    {"pts": pt(k)},
                )
            )
        out_ref[:, spot] = sums[g, p]

    for g in range(share_tiles // group):
        finish(g)
    copies += [
        remote(log_all.at[p], log_all.at[p], log_send.at[k], log_recv.at[k], {"pts": pt(k)})
        for k in order
    ]
    for copy in copies:
        copy.wait_recv()
    for s in range(n):
        log_ref[s * share_tiles : (s + 1) * share_tiles, :] = log_all[s, :share_tiles, :]
    for copy in started + copies:
        copy.wait_send()


def hand_on(out_in, log_in, out_ref, log_ref, sem):
    rows = out_in.shape[0] // 8
    copies = [
        pltpu.make_async_copy(
            out_in.at[8 * i : 8 * i + 8], out_ref.at[8 * i : 8 * i + 8], sem.at[i]
        )
        for i in range(rows)
    ]
    copies.append(pltpu.make_async_copy(log_in, log_ref, sem.at[rows]))
    for copy in copies:
        copy.start()
    for copy in copies:
        copy.wait()


def local(n, nl, points, centroids, prior, loads):
    m, dim = points.shape
    lists = centroids.shape[0]
    tiles = lists // LANES
    chunks = m // LANES
    share = lists // n
    scale = (m * n) / (8.0 * lists * nl)
    paced = n == 8
    group = min(2, share // LANES)
    f32 = jnp.float32
    dma = pltpu.SemaphoreType.DMA
    out, log = pl.pallas_call(
        functools.partial(kernel, n, nl, scale, paced, group),
        out_shape=(
            jax.ShapeDtypeStruct((dim // n, lists), f32),
            jax.ShapeDtypeStruct((tiles, LANES), f32),
        ),
        in_specs=[
            pl.BlockSpec(memory_space=pltpu.VMEM),
            pl.BlockSpec(memory_space=pl.ANY),
            pl.BlockSpec(memory_space=pltpu.VMEM),
            pl.BlockSpec(memory_space=pltpu.VMEM),
        ],
        out_specs=[pl.BlockSpec(memory_space=pltpu.VMEM)] * 2,
        scratch_shapes=[
            pltpu.VMEM((tiles, m, LANES), f32),
            pltpu.VMEM((n * chunks, share, LANES), f32),
            pltpu.VMEM((n, m + 8, dim), f32),
            pltpu.VMEM((dim, n * m), jnp.bfloat16),
            pltpu.VMEM((share, n * m), jnp.bfloat16),
            pltpu.VMEM((m, LANES), f32),
            pltpu.VMEM((m, LANES), f32),
            pltpu.VMEM((m, LANES), f32),
            pltpu.VMEM((tiles, LANES), f32),
            pltpu.VMEM((ITERS, 8, LANES), f32),
            pltpu.VMEM((ITERS, nl, 8, LANES), f32),
            pltpu.VMEM((ITERS - 1, tiles, LANES), f32),
            pltpu.VMEM((ITERS - 1, n, tiles, LANES), f32),
            pltpu.VMEM((n, 8, LANES), f32),
            pltpu.VMEM((share // LANES // group, n, dim // n, group * LANES), f32),
            pltpu.VMEM((n, 8, LANES), f32),
            dma((ITERS, nl)),
            dma((ITERS, nl)),
            dma((ITERS - 1, n)),
            dma((ITERS - 1, n)),
            dma((max(n // 2, 7),)),
            dma((max(n // 2, 7),)),
            dma((n // 2,)),
            dma((n // 2,)),
            dma((n,)),
            dma((n,)),
            dma((share // LANES // group, n)),
            dma((share // LANES // group, n)),
            dma((n,)),
            dma((n,)),
            pltpu.VMEM((lists, dim), jnp.bfloat16),
            dma,
        ],
        compiler_params=pltpu.CompilerParams(
            collective_id=0, has_side_effects=True, vmem_limit_bytes=56 * 1024 * 1024
        ),
    )(points, centroids, prior.reshape(chunks, LANES), loads.reshape(tiles, LANES))
    out, log = pl.pallas_call(
        hand_on,
        out_shape=(
            jax.ShapeDtypeStruct(out.shape, f32),
            jax.ShapeDtypeStruct(log.shape, f32),
        ),
        in_specs=[pl.BlockSpec(memory_space=pl.ANY)] * 2,
        out_specs=[pl.BlockSpec(memory_space=pl.ANY)] * 2,
        scratch_shapes=[dma((dim // n // 8 + 1,))],
    )(out, log)
    return out, log.reshape(lists)


def solution(mesh):
    return jax.shard_map(
        functools.partial(local, mesh.shape["pts"], mesh.shape["lists"]),
        mesh=mesh,
        in_specs=(P("pts", None), P("lists", None), P("pts"), P("lists")),
        out_specs=(P("pts", "lists"), P("lists")),
        check_vma=False,
    )
```

```python
import functools

import jax
import jax.numpy as jnp
from jax import lax
from jax.experimental import pallas as pl
from jax.experimental.pallas import tpu as pltpu

from jax.sharding import PartitionSpec as P

ITERS = 3
BLOCK = 512
LANES = 128
MESH = pl.DeviceIdType.MESH
NT = (((1,), (1,)), ((), ()))


def spread(row):
    return jnp.broadcast_to(row, (LANES, LANES)).T


def gather_up(block):
    return jnp.sum(block.T, axis=0, keepdims=True)


def kernel(
    n,
    nl,
    scale,
    paced,
    group,
    pts_ref,
    cent_hbm,
    prior_ref,
    loads_ref,
    out_ref,
    log_ref,
    mass,
    mass_t,
    allp,
    pts_t,
    plan_t,
    near,
    rowb,
    rowacc,
    col,
    row_out,
    row_in,
    col_out,
    col_in,
    row_all,
    sums,
    log_all,
    row_send,
    row_recv,
    col_send,
    col_recv,
    ag_send,
    ag_recv,
    fw_send,
    fw_recv,
    ra_send,
    ra_recv,
    out_send,
    out_recv,
    log_send,
    log_recv,
    cent_ref,
    cent_sem,
):
    p = lax.axis_index("pts")
    z = lax.axis_index("lists")
    m = pts_ref.shape[0]
    lists = cent_ref.shape[0]
    tiles = lists // LANES
    chunks = m // LANES
    share = lists // n
    share_tiles = share // LANES
    half = n // 2
    sibling = p + 1 - 2 * lax.rem(p, 2)

    def pt(k):
        return lax.rem(p + k, n)

    fetch = pltpu.make_async_copy(cent_hbm, cent_ref, cent_sem)
    fetch.start()
    barrier = pltpu.get_barrier_semaphore()
    for k in range(1, n):
        pl.semaphore_signal(barrier, inc=1, device_id={"pts": pt(k)}, device_id_type=MESH)
    for k in range(1, nl):
        pl.semaphore_signal(
            barrier, inc=1, device_id={"lists": lax.rem(z + k, nl)}, device_id_type=MESH
        )

    allp[p, :m, :] = pts_ref[...].astype(jnp.float32)
    allp[p, m:, :] = jnp.zeros((8, allp.shape[2]), jnp.float32)
    row_out[...] = jnp.zeros_like(row_out)
    log_all[p] = jnp.zeros(log_all.shape[1:], jnp.float32)
    for r in range(chunks):
        prior_row = prior_ref[r : r + 1, :].astype(jnp.float32)
        allp[p, m + r : m + r + 1, 0:LANES] = prior_row
        near[r * LANES : (r + 1) * LANES, :] = spread(prior_row - (z * lists).astype(jnp.float32))
    pl.semaphore_wait(barrier, n - 1 + nl - 1)

    def remote(src, dst, send, recv, where):
        copy = pltpu.make_async_remote_copy(
            src_ref=src, dst_ref=dst, send_sem=send, recv_sem=recv,
            device_id=where, device_id_type=MESH,
        )
        copy.start()
        return copy

    started = []

    def send_piece(source, rows, send, recv, where):
        copy = remote(allp.at[source, rows], allp.at[source, rows], send, recv, {"pts": where})
        started.append(copy)
        return copy

    whole = pl.ds(0, m + 8)
    near_sib = send_piece(p, whole, ag_send.at[0], ag_recv.at[0], sibling)
    if paced:
        over_x = p + 2 - 4 * lax.rem(p // 2, 2)
        over_y = p + 4 - 8 * lax.rem(p // 4, 2)
        across = over_x + 4 - 8 * lax.rem(p // 4, 2)
        first_rows, last_rows = pl.ds(0, m // 2), pl.ds(m // 2, m // 2 + 8)
        head = [
            send_piece(p, first_rows, ag_send.at[1], ag_recv.at[1], over_x),
            send_piece(p, first_rows, ag_send.at[2], ag_recv.at[2], over_y),
        ]
    else:
        gathers = [
            send_piece(p, whole, ag_send.at[k], ag_recv.at[k], pt(2 * k)) for k in range(1, half)
        ]

    rowacc[...] = jnp.zeros_like(rowacc)
    per = BLOCK // LANES
    lane = lax.broadcasted_iota(jnp.int32, (m, LANES), 1).astype(jnp.float32)

    def make(b, carry):
        score = lax.dot_general(
            pts_ref[...], cent_ref[pl.ds(pl.multiple_of(b * BLOCK, BLOCK), BLOCK), :], NT,
            preferred_element_type=jnp.float32,
        )
        rel = near[...] - (b * BLOCK).astype(jnp.float32)
        total = rowacc[...]
        for c in range(per):
            hit = jnp.where(rel == lane + float(c * LANES), 10.0, 0.0)
            value = jnp.exp(3.0 * score[:, c * LANES : (c + 1) * LANES] + hit)
            mass[b * per + c] = value
            total = total + value
        rowacc[...] = total
        return carry

    fetch.wait()
    lax.fori_loop(0, lists // BLOCK, make, 0)

    def send_rows(step):
        for r in range(chunks):
            row_out[step, r : r + 1, :] = gather_up(rowacc[r * LANES : (r + 1) * LANES, :])
        copies = [
            remote(
                row_out.at[step], row_in.at[step, k], row_send.at[step, k], row_recv.at[step, k],
                {"lists": lax.rem(z + k, nl)},
            )
            for k in range(1, nl)
        ]
        started.extend(copies)
        return copies

    def take_rows(step, copies):
        total = row_out[step]
        for k, copy in enumerate(copies, 1):
            copy.wait_recv()
            total = total + row_in[step, k]
        return 1.0 / total

    def send_cols(step, row):
        for r in range(chunks):
            rowb[r * LANES : (r + 1) * LANES, :] = spread(row[r : r + 1, :])

        def add(t, carry):
            col_out[step, pl.ds(t, 1), :] = jnp.sum(mass[t] * rowb[...], axis=0, keepdims=True)
            return carry

        lax.fori_loop(0, tiles, add, 0, unroll=4)
        copies = [
            remote(
                col_out.at[step], col_in.at[step, k], col_send.at[step, k], col_recv.at[step, k],
                {"pts": pt(k)},
            )
            for k in range(1, n)
        ]
        started.extend(copies)
        return copies

    def take_cols(step, copies):
        total = col_out[step]
        for k, copy in enumerate(copies, 1):
            copy.wait_recv()
            total = total + col_in[step, k]
        col[...] = loads_ref[...].astype(jnp.float32) * scale / total

    def add_rows():
        for r in range(chunks):
            part = pl.ds(r * LANES, LANES)

            def add(t, acc):
                return acc + mass[t, part, :] * col[pl.ds(t, 1), :]

            rowacc[part, :] = lax.fori_loop(
                0, tiles, add, jnp.zeros((LANES, LANES), jnp.float32), unroll=4
            )

    own = pl.multiple_of(p * share, share)
    first = (z * lists + p * share).astype(jnp.float32)
    index = lax.broadcasted_iota(jnp.int32, (share, LANES), 0).astype(jnp.float32) + first

    def part_of(s):
        piece = allp[s, :m, :]
        pts_t[:, pl.ds(pl.multiple_of(s * m, LANES), m)] = piece.T.astype(jnp.bfloat16)
        score = lax.dot_general(
            cent_ref[pl.ds(own, share), :], piece.astype(jnp.bfloat16), NT,
            preferred_element_type=jnp.float32,
        )
        for r in range(chunks):
            hit = jnp.where(index == allp[s, m + r : m + r + 1, 0:LANES], 10.0, 0.0)
            mass_t[s * chunks + r] = jnp.exp(3.0 * score[:, r * LANES : (r + 1) * LANES] + hit)

    copies = send_rows(0)
    part_of(p)
    row = take_rows(0, copies)
    copies = send_cols(0, row)
    near_sib.wait_recv()
    part_of(sibling)
    take_cols(0, copies)
    if paced:
        tail = [
            send_piece(p, last_rows, ag_send.at[3], ag_recv.at[3], over_x),
            send_piece(p, last_rows, ag_send.at[4], ag_recv.at[4], over_y),
        ]
    add_rows()
    row = take_rows(1, send_rows(1))
    take_cols(1, send_cols(1, row))
    if paced:
        for copy in head + tail:
            copy.wait_recv()
        on = [
            send_piece(over_x, first_rows, ag_send.at[5], ag_recv.at[5], over_y),
            send_piece(over_y, last_rows, ag_send.at[6], ag_recv.at[6], over_x),
        ]
        forwards = [
            send_piece(over_x, whole, fw_send.at[1], fw_recv.at[1], sibling),
            send_piece(over_y, whole, fw_send.at[2], fw_recv.at[2], sibling),
        ]
    add_rows()
    copies = send_rows(2)
    if not paced:
        forwards = []
        for k in range(1, half):
            gathers[k - 1].wait_recv()
            source = pt(n - 2 * k)
            forwards.append(send_piece(source, whole, fw_send.at[k], fw_recv.at[k], sibling))
    row_all[p] = take_rows(2, copies)
    copies = [
        remote(row_all.at[p], row_all.at[p], ra_send.at[k], ra_recv.at[k], {"pts": pt(k)})
        for k in range(1, n)
    ]
    started += copies
    if paced:

        def pair(first, second):
            def one(k, carry):
                part_of(first + k * (second - first))
                return carry

            lax.fori_loop(0, 2, one, 0)

        pair(over_x, over_y)
        for copy in on:
            copy.wait_recv()
        forwards.append(send_piece(across, whole, fw_send.at[3], fw_recv.at[3], sibling))
        for copy in forwards[:2]:
            copy.wait_recv()
        across_sib = across + 1 - 2 * lax.rem(p, 2)
        pair(over_x + sibling - p, over_y + sibling - p)
        part_of(across)
        forwards[2].wait_recv()
        part_of(across_sib)
    else:

        def direct(k, carry):
            part_of(lax.rem(p + n - 2 * k, n))
            return carry

        lax.fori_loop(1, half, direct, 0)
        for copy in forwards:
            copy.wait_recv()

        def relayed(k, carry):
            part_of(lax.rem(sibling + n - 2 * k, n))
            return carry

        lax.fori_loop(1, half, relayed, 0)
    for copy in copies:
        copy.wait_recv()

    depth = out_ref.shape[0]
    order = [k for k in range(1, n)][::-1]
    copies = []

    def finish(g):
        width = group * LANES
        for c in range(g * group, (g + 1) * group):
            part = pl.ds(c * LANES, LANES)

            def add(s, acc):
                for r in range(chunks):
                    acc = acc + mass_t[s * chunks + r, part, :] * row_all[s, r : r + 1, :]
                return acc

            acc = lax.fori_loop(0, n, add, jnp.zeros((LANES, LANES), jnp.float32), unroll=2)
            total = jnp.sum(acc, axis=1, keepdims=True)
            target = loads_ref[pl.ds(p * share_tiles + c, 1), :].astype(jnp.float32) * scale
            colb = spread(target) / total
            log_all[p, c : c + 1, :] = jnp.log(colb).T[0:1, :]

            def plan(s, carry):
                for r in range(chunks):
                    value = mass_t[s * chunks + r, part, :] * row_all[s, r : r + 1, :] * colb
                    spot = pl.ds(pl.multiple_of(s * m + r * LANES, LANES), LANES)
                    plan_t[part, spot] = value.astype(jnp.bfloat16)
                return carry

            lax.fori_loop(0, n, plan, 0, unroll=2)
        total = lax.dot_general(
            pts_t[...], plan_t[g * width : (g + 1) * width, :], NT,
            preferred_element_type=jnp.float32,
        )
        for c in range(group):
            target = loads_ref[
                pl.ds(p * share_tiles + g * group + c, 1), :
            ].astype(jnp.float32) * scale
            part = total[:, c * LANES : (c + 1) * LANES] * (1.0 / target)
            for q in range(n):
                sums[g, q, :, c * LANES : (c + 1) * LANES] = part[q * depth : (q + 1) * depth, :]
        spot = pl.ds(pl.multiple_of(p * share + g * width, LANES), width)
        for k in order:
            copies.append(
                remote(
                    sums.at[g, pt(k)], out_ref.at[:, spot], out_send.at[g, k], out_recv.at[g, k],
                    {"pts": pt(k)},
                )
            )
        out_ref[:, spot] = sums[g, p]

    for g in range(share_tiles // group):
        finish(g)
    copies += [
        remote(log_all.at[p], log_all.at[p], log_send.at[k], log_recv.at[k], {"pts": pt(k)})
        for k in order
    ]
    for copy in copies:
        copy.wait_recv()
    for s in range(n):
        log_ref[s * share_tiles : (s + 1) * share_tiles, :] = log_all[s, :share_tiles, :]
    for copy in started + copies:
        copy.wait_send()


def hand_on(out_in, log_in, out_ref, log_ref, out_held, log_held, in_sem, out_sem):
    rows = [pl.ds(8 * i, 8) for i in range(out_in.shape[0] // 8)]
    stages = [(out_in.at[r], out_held.at[r], out_ref.at[r]) for r in rows]
    stages.append((log_in, log_held, log_ref))
    fetches, stores = [], []
    for i, (source, held, dest) in enumerate(stages):
        fetches.append(pltpu.make_async_copy(source, held, in_sem.at[i]))
        stores.append(pltpu.make_async_copy(held, dest, out_sem.at[i]))
    for copy in fetches:
        copy.start()
    for fetch, store in zip(fetches, stores):
        fetch.wait()
        store.start()
    for copy in stores:
        copy.wait()


def local(n, nl, points, centroids, prior, loads):
    m, dim = points.shape
    lists = centroids.shape[0]
    tiles = lists // LANES
    chunks = m // LANES
    share = lists // n
    scale = (m * n) / (8.0 * lists * nl)
    paced = n == 8
    group = min(2, share // LANES)
    f32 = jnp.float32
    dma = pltpu.SemaphoreType.DMA
    out, log = pl.pallas_call(
        functools.partial(kernel, n, nl, scale, paced, group),
        out_shape=(
            jax.ShapeDtypeStruct((dim // n, lists), f32),
            jax.ShapeDtypeStruct((tiles, LANES), f32),
        ),
        in_specs=[
            pl.BlockSpec(memory_space=pltpu.VMEM),
            pl.BlockSpec(memory_space=pl.ANY),
            pl.BlockSpec(memory_space=pltpu.VMEM),
            pl.BlockSpec(memory_space=pltpu.VMEM),
        ],
        out_specs=[pl.BlockSpec(memory_space=pltpu.VMEM)] * 2,
        scratch_shapes=[
            pltpu.VMEM((tiles, m, LANES), f32),
            pltpu.VMEM((n * chunks, share, LANES), f32),
            pltpu.VMEM((n, m + 8, dim), f32),
            pltpu.VMEM((dim, n * m), jnp.bfloat16),
            pltpu.VMEM((share, n * m), jnp.bfloat16),
            pltpu.VMEM((m, LANES), f32),
            pltpu.VMEM((m, LANES), f32),
            pltpu.VMEM((m, LANES), f32),
            pltpu.VMEM((tiles, LANES), f32),
            pltpu.VMEM((ITERS, 8, LANES), f32),
            pltpu.VMEM((ITERS, nl, 8, LANES), f32),
            pltpu.VMEM((ITERS - 1, tiles, LANES), f32),
            pltpu.VMEM((ITERS - 1, n, tiles, LANES), f32),
            pltpu.VMEM((n, 8, LANES), f32),
            pltpu.VMEM((share // LANES // group, n, dim // n, group * LANES), f32),
            pltpu.VMEM((n, 8, LANES), f32),
            dma((ITERS, nl)),
            dma((ITERS, nl)),
            dma((ITERS - 1, n)),
            dma((ITERS - 1, n)),
            dma((max(n // 2, 7),)),
            dma((max(n // 2, 7),)),
            dma((n // 2,)),
            dma((n // 2,)),
            dma((n,)),
            dma((n,)),
            dma((share // LANES // group, n)),
            dma((share // LANES // group, n)),
            dma((n,)),
            dma((n,)),
            pltpu.VMEM((lists, dim), jnp.bfloat16),
            dma,
        ],
        compiler_params=pltpu.CompilerParams(
            collective_id=0, has_side_effects=True, vmem_limit_bytes=56 * 1024 * 1024
        ),
    )(points, centroids, prior.reshape(chunks, LANES), loads.reshape(tiles, LANES))
    out, log = pl.pallas_call(
        hand_on,
        out_shape=(
            jax.ShapeDtypeStruct(out.shape, f32),
            jax.ShapeDtypeStruct(log.shape, f32),
        ),
        in_specs=[pl.BlockSpec(memory_space=pl.ANY)] * 2,
        out_specs=[pl.BlockSpec(memory_space=pl.ANY)] * 2,
        scratch_shapes=[
            pltpu.VMEM(out.shape, f32),
            pltpu.VMEM(log.shape, f32),
            dma((dim // n // 8 + 1,)),
            dma((dim // n // 8 + 1,)),
        ],
    )(out, log)
    return out, log.reshape(lists)


def solution(mesh):
    return jax.shard_map(
        functools.partial(local, mesh.shape["pts"], mesh.shape["lists"]),
        mesh=mesh,
        in_specs=(P("pts", None), P("lists", None), P("pts"), P("lists")),
        out_specs=(P("pts", "lists"), P("lists")),
        check_vma=False,
    )
```
